256 devices in a mesh: lat: 16 (over x, y), lev: 16 (over z, core).
Axes of the slice: x: 4, y: 4, z: 8, core: 2. Of those that a mesh axis runs over, the one named last changes fastest.
Arguments:
- grid: bfloat16 [64, 1280, 2560], P('lev', 'lat'), may hold values from -6 to 6
- pair_index: int32 [512], replicated, may hold values from 1 to 639, as said below
- legendre: bfloat16 [512, 1280, 1280], P('lev', 'lat'), may hold values from -0.15625 to 0.15625
- vertical: bfloat16 [64, 64], replicated, may hold values from -0.75 to 0.75
Outputs:
- spectral: bfloat16 [16, 32, 1280, 128], P('lev', 'lat')
The draws below stay inside these ranges and needn't reach their ends.
Inputs may be any that keep to these rules, and one draw needn't show every extreme that they name: `pair_index`: distinct pair numbers; pair p holds wavenumbers p and 1280 - p.
All inputs are finite; a program needn't handle non-finite values.
Results may differ from the reference program's by a relative error of at most 0.017.
Values may be sent and summed in bfloat16 or wider, within the bound.
A program may use at most 192 MiB of HBM per device.

```python
import math
import jax
import jax.numpy as jnp
from jax import lax

NLON = 2560
NLAT = 1280
NDEG = 1280
ROWS = 1280
LEVELS = 64
PAIR_DEV = 2
PAIRS = 512
N_LAT = 16
N_LEV = 16


def draw_pair_index(key, part):
    key = jax.random.fold_in(key, 7)
    first, second = jax.random.split(key)
    inner = 2 + jax.random.permutation(first, NDEG // 2 - 3)[:PAIRS - 2]
    ends = jnp.array([1, NDEG // 2 - 1], dtype=jnp.int32)
    values = jnp.concatenate([ends, inner.astype(jnp.int32)])
    return values[jax.random.permutation(second, PAIRS)]


def level_of(key, dims, pieces, low, high):
    factor_of, own = 1.0, jax.random.fold_in(key, 6)
    for dim, blocks in pieces:
        steps = jnp.exp(jax.random.uniform(jax.random.fold_in(own, dim), (blocks,), jnp.float32, low / len(pieces), high / len(pieces)))
        factor_of = factor_of * jnp.repeat(steps, dims[dim] // blocks).reshape([-1 if axis == dim else 1 for axis in range(len(dims))])
    return factor_of


def noise(rng, dims, width, most, pieces=(), held_as=jnp.bfloat16):
    values = jax.random.normal(rng, dims, jnp.float32) * width
    if len(pieces) > 0:
        values = level_of(rng, dims, pieces, -0.22, 0.18) * values
    return jnp.clip(values, min=-most, max=most).astype(held_as)


def setup_inputs(seed: int = 0) -> dict:
    seeds = jax.random.split(jax.random.key(seed), 5)
    return {
        "grid": noise(seeds[0], (LEVELS, NLAT, NLON), 1.0, 6.0, ((0, 16), (1, 16))),
        "pair_index": draw_pair_index(jax.random.fold_in(seeds[4], 71), 0),
        "legendre": noise(seeds[2], (PAIRS, NLAT, ROWS), NLAT ** -0.5, 0.15625, ((0, 16), (1, 16))),
        "vertical": noise(seeds[3], (LEVELS, LEVELS), LEVELS ** -0.5, 0.75),
    }


def fourier_table(pair_index):
    wavenumbers = jnp.stack([pair_index, NDEG - pair_index], axis=1).astype(jnp.int32)
    longitude = jnp.arange(NLON, dtype=jnp.int32)
    phase = longitude[:, None, None] * wavenumbers[None, :, :] % NLON
    angle = phase.astype(jnp.float32) * jnp.float32(2.0 * math.pi / NLON)
    factor = jnp.float32(1.0 / math.sqrt(NLON))
    table = jnp.stack([jnp.cos(angle) * factor, -jnp.sin(angle) * factor], axis=-1)
    return table.reshape(NLON, PAIRS * 4).astype(jnp.bfloat16)

def reference(grid, pair_index, legendre, vertical):
    table = fourier_table(pair_index)
    fourier = jnp.dot(grid.reshape(LEVELS * NLAT, NLON), table, preferred_element_type=jnp.float32)
    fourier = fourier.astype(jnp.bfloat16).reshape(LEVELS, NLAT, PAIRS, 2, 2)
    by_slot = jnp.moveaxis(fourier, 2, 0)
    row_ids = jnp.arange(ROWS, dtype=jnp.int32)
    vertical_f = vertical.astype(jnp.float32)

    def one_slot(items):
        rows_table, slot_four, pair = items
        both = jnp.einsum('kr,lkuc->urcl', rows_table.astype(jnp.float32), slot_four.astype(jnp.float32))
        first = row_ids < NDEG - pair
        coef = jnp.where(first[:, None, None], both[0], both[1]).astype(jnp.bfloat16)
        mixed = jnp.einsum('rcl,ml->rcm', coef.astype(jnp.float32), vertical_f)
        return mixed.astype(jnp.bfloat16).reshape(ROWS, 2 * LEVELS)
    result = lax.map(one_slot, (legendre, by_slot, pair_index))
    return result.reshape(N_LEV, N_LAT * PAIR_DEV, ROWS, 2 * LEVELS)
```

```python
import functools
import math

import jax
import jax.numpy as jnp
from jax import lax
from jax.sharding import PartitionSpec as P
from jax.experimental import pallas as pl
from jax.experimental.pallas import tpu as pltpu

MESH = pl.DeviceIdType.MESH
F32 = jnp.float32
BF16 = jnp.bfloat16
NLON = 2560
NDEG = 1280
ROWS = 1280
LOW = 64
HIGH = NLON // LOW
DIST = (2, 1, 3, 0)


def iota(shape, dim):
    return lax.broadcasted_iota(jnp.int32, shape, dim)


def cos_sin(turns_num):
    whole = jnp.floor(turns_num * F32(1.0 / NLON) + F32(0.5))
    h = (turns_num - whole * F32(NLON)) * F32(math.pi / NLON)
    h2 = h * h
    s = F32(-1.0 / 39916800.0)
    for c in (1.0 / 362880.0, -1.0 / 5040.0, 1.0 / 120.0, -1.0 / 6.0, 1.0):
        s = s * h2 + F32(c)
    s = s * h
    c_ = F32(1.0 / 479001600.0)
    for c in (-1.0 / 3628800.0, 1.0 / 40320.0, -1.0 / 720.0, 1.0 / 24.0, -0.5, 1.0):
        c_ = c_ * h2 + F32(c)
    return F32(1.0) - F32(2.0) * s * s, F32(2.0) * s * c_


def kernel(pair_ref, leg, grid_hbm, pcol, vert, out,
           grid, gsign, table, base_a, base_b, base_c, base_s, xs, xr, perm, zs, zr,
           wide, mixed, leg1, leg2, rs, rr,
           grid_sem, legl_sem, legs_sem, legr_sem, xs_sem, xr_sem, zl_sem, zs_sem, zr_sem, rs_sem, rr_sem):
    lat = lax.axis_index("lat")
    lev = lax.axis_index("lev")
    x, y = lat // 4, lat % 4

    def at_x(d):
        return (lax.rem(x + d, 4) * 4 + y, lev)

    def at_y(d):
        return (x * 4 + lax.rem(y + d, 4), lev)

    def at_z(e):
        return (lat, lax.rem(lev + e, 16))

    barrier = pltpu.get_barrier_semaphore()
    peers = [at_x(d) for d in (1, 2, 3)] + [at_y(d) for d in (1, 2, 3)] + [at_z(e) for e in range(1, 16)]
    for peer in peers:
        pl.semaphore_signal(barrier, inc=1, device_id=peer, device_id_type=MESH)

    grid_copy = pltpu.make_async_copy(grid_hbm, grid, grid_sem)
    grid_copy.start()

    local = []
    for n, d in enumerate(DIST):
        sy, sx = lax.rem(y + d, 4), lax.rem(x + d, 4)
        local.append((
            pltpu.make_async_copy(leg.at[x, sy, 0], leg1.at[sy, pl.ds(x * 5, 5)], legl_sem.at[0, d]),
            pltpu.make_async_copy(leg.at[sx, y, 1], leg2.at[sx, pl.ds(4 + y * 5, 5)], legl_sem.at[1, d]),
        ))
    for pair in local:
        for copy in pair:
            copy.start()
    leg1[:, 20:24] = jnp.zeros((4, 4, 16, ROWS), BF16)
    leg2[:, 0:4] = jnp.zeros((4, 4, 16, ROWS), BF16)

    remote = []
    for d in DIST:
        sy, sx = lax.rem(y + d, 4), lax.rem(x + d, 4)
        group = []
        for e in (2, 1, 3):
            px, py = lax.rem(x + e, 4), lax.rem(y + e, 4)
            group.append(pltpu.make_async_remote_copy(
                src_ref=leg.at[px, sy, 0], dst_ref=leg1.at[sy, pl.ds(x * 5, 5)],
                send_sem=legs_sem.at[0, d, e], recv_sem=legr_sem.at[0, d, e],
                device_id=at_x(e), device_id_type=MESH))
            group.append(pltpu.make_async_remote_copy(
                src_ref=leg.at[sx, py, 1], dst_ref=leg2.at[sx, pl.ds(4 + y * 5, 5)],
                send_sem=legs_sem.at[1, d, e], recv_sem=legr_sem.at[1, d, e],
                device_id=at_y(e), device_id_type=MESH))
        remote.append(group)

    row, col = iota((256, 256), 0), iota((256, 256), 1)
    want = ((row // 8) % 2) * 128 + (row // 16) * 8 + row % 8
    sign = jnp.where(((row // 8) % 2 == 1) & (row % 2 == 1), F32(-1.0), F32(1.0))
    perm[...] = jnp.where(col == want, sign, F32(0.0)).astype(BF16)

    def make_base(d, h):
        dest = lax.rem((x if h == 0 else y) + d, 4)
        p = pcol[h, dest]
        low = iota((LOW, 128), 0).astype(F32)
        cos, sin = cos_sin(low * p)
        base_c[...] = cos
        base_s[...] = sin
        high = (iota((HIGH, 128), 0) * LOW).astype(F32)
        cos, sin = cos_sin(high * p)
        imag = iota((HIGH, 128), 1) % 2 == 1
        factor = F32(1.0 / math.sqrt(NLON))
        base_a[...] = jnp.where(imag, -sin, cos) * factor
        base_b[...] = jnp.where(imag, -cos, -sin) * factor

    def make_table(d):
        for h in range(2):
            make_base(d, h)

            @pl.loop(0, HIGH // 8)
            def _(g):
                a = base_a[pl.ds(pl.multiple_of(g * 8, 8), 8)]
                b = base_b[pl.ds(pl.multiple_of(g * 8, 8), 8)]
                for i in range(8):
                    block = a[i:i + 1] * base_c[...] + b[i:i + 1] * base_s[...]
                    first = pl.multiple_of((g * 8 + i) * LOW, LOW)
                    table[pl.ds(first, LOW), h * 128:(h + 1) * 128] = block.astype(BF16)

    make_table(DIST[0])
    grid_copy.wait()
    odd = iota((320, NLON), 1) % 2 == 1
    flat = grid[...].reshape(320, NLON)
    gsign[...] = jnp.where(odd, -flat, flat)

    pl.semaphore_wait(barrier, len(peers))
    for copy in remote[0]:
        copy.start()

    x_copies = []
    for n, d in enumerate(DIST):
        if n > 0:
            make_table(d)
        for u in range(2):
            source = grid[...].reshape(320, NLON) if u == 0 else gsign[...]
            four = jnp.dot(source, table[...], preferred_element_type=F32).astype(BF16)
            for h in range(2):
                part = four[:, h * 128:(h + 1) * 128].reshape(4, 80, 128)
                if d == 0:
                    own = x if h == 0 else 4 + y
                    xr[:, own, :, u * 128:(u + 1) * 128] = part
                else:
                    xs[d - 1, h, :, :, u * 128:(u + 1) * 128] = part
        if d > 0:
            for h in range(2):
                copy = pltpu.make_async_remote_copy(
                    src_ref=xs.at[d - 1, h], dst_ref=xr.at[:, x if h == 0 else 4 + y],
                    send_sem=xs_sem.at[h, d], recv_sem=xr_sem.at[h, d],
                    device_id=at_x(d) if h == 0 else at_y(d), device_id_type=MESH)
                copy.start()
                x_copies.append(copy)
    for copy in remote[1]:
        copy.start()

    level_of = (iota((64, 1024), 1) // 16 == iota((64, 1024), 0)).astype(BF16)
    spread = jnp.dot(vert[...], level_of, preferred_element_type=F32)
    inner = iota((64, 1024), 1) % 16
    for s in range(4):
        for u in range(2):
            for c in range(2):
                i = s * 4 + u * 2 + c
                wide[i * 64:(i + 1) * 64, :] = jnp.where(inner == u * 8 + s * 2 + c, spread, F32(0.0)).astype(BF16)

    for copy in x_copies:
        copy.wait()
    for l in range(4):
        turned = lax.dot_general(perm[...], xr[l].reshape(640, 256), (((1,), (1,)), ((), ())),
                                 preferred_element_type=F32).astype(BF16)
        zs[:, l] = turned.reshape(16, 16, 640)
    z_copies = []
    for e in (8, 7, 9, 6, 10, 5, 11, 4, 12, 3, 13, 2, 14, 1, 15):
        copy = pltpu.make_async_remote_copy(
            src_ref=zs.at[lax.rem(lev + e, 16)], dst_ref=zr.at[lev],
            send_sem=zs_sem.at[e], recv_sem=zr_sem.at[e],
            device_id=at_z(e), device_id_type=MESH)
        copy.start()
        z_copies.append(copy)
    z_own = pltpu.make_async_copy(zs.at[lev], zr.at[lev], zl_sem)
    z_own.start()
    for group in remote[2:]:
        for copy in group:
            copy.start()
    z_own.wait()
    for copy in z_copies:
        copy.wait()
    mixed[...] = jnp.dot(wide[...], zr[...].reshape(1024, 640), preferred_element_type=F32).astype(BF16)

    out_copies = []
    for n, d in enumerate(DIST):
        for copy in local[n]:
            copy.wait()
        for copy in remote[n]:
            copy.wait()
        for h in range(2):
            s = lax.rem((y if h == 0 else x) + d, 4)
            slot = lev * 32 + (x * 4 + s) * 2 if h == 0 else lev * 32 + (s * 4 + y) * 2 + 1
            p = pair_ref[slot]
            legs = leg1 if h == 0 else leg2
            lanes = slice(0, 384) if h == 0 else slice(256, 640)
            g = mixed[pl.ds(pl.multiple_of(s * 256, 256), 256), lanes]
            half = ROWS // 2
            left = jnp.dot(g[0:128], legs[s, :, :, 0:half].reshape(384, half), preferred_element_type=F32)
            both = jnp.dot(g, legs[s, :, :, half:ROWS].reshape(384, half), preferred_element_type=F32)
            first = iota((128, half), 1) + half < NDEG - p
            right = jnp.where(first, both[0:128], both[128:256])
            dest = rr.at[h, 0] if d == 0 else rs.at[h, d - 1]
            dest[:, 0:half] = left.astype(BF16)
            dest[:, half:ROWS] = right.astype(BF16)
            if d > 0:
                copy = pltpu.make_async_remote_copy(
                    src_ref=rs.at[h, d - 1], dst_ref=rr.at[h, d],
                    send_sem=rs_sem.at[h, d], recv_sem=rr_sem.at[h, d],
                    device_id=at_y(d) if h == 0 else at_x(d), device_id_type=MESH)
                copy.start()
                out_copies.append(copy)
    for copy in out_copies:
        copy.wait()
    for h in range(2):
        for r in range(0, ROWS, 256):
            total = rr[h, 0, :, r:r + 256].astype(F32)
            for d in (1, 2, 3):
                total = total + rr[h, d, :, r:r + 256].astype(F32)
            out[0, h, r:r + 256, :] = total.T.astype(BF16)


def body(grid, pair_index, legendre, vertical):
    slots = pair_index.reshape(16, 4, 4, 2)
    over_x = slots[:, :, :, 0].transpose(1, 0, 2).reshape(4, 64)
    over_y = slots[:, :, :, 1].transpose(2, 0, 1).reshape(4, 64)
    pcol = jnp.repeat(jnp.stack([over_x, over_y]), 2, axis=-1).astype(F32).reshape(2, 4, 1, 128)
    vmem = pl.BlockSpec(memory_space=pltpu.VMEM)
    hbm = pl.BlockSpec(memory_space=pl.ANY)
    dma = pltpu.SemaphoreType.DMA
    return pl.pallas_call(
        kernel,
        out_shape=jax.ShapeDtypeStruct((1, 2, ROWS, 128), BF16),
        in_specs=[pl.BlockSpec(memory_space=pltpu.SMEM), hbm, hbm, vmem, vmem],
        out_specs=vmem,
        scratch_shapes=[
            pltpu.VMEM((4, 80, NLON), BF16),
            pltpu.VMEM((320, NLON), BF16),
            pltpu.VMEM((NLON, 256), BF16),
            pltpu.VMEM((HIGH, 128), F32),
            pltpu.VMEM((HIGH, 128), F32),
            pltpu.VMEM((LOW, 128), F32),
            pltpu.VMEM((LOW, 128), F32),
            pltpu.VMEM((3, 2, 4, 80, 256), BF16),
            pltpu.VMEM((4, 8, 80, 256), BF16),
            pltpu.VMEM((256, 256), BF16),
            pltpu.VMEM((16, 4, 16, 640), BF16),
            pltpu.VMEM((16, 4, 16, 640), BF16),
            pltpu.VMEM((1024, 1024), BF16),
            pltpu.VMEM((1024, 640), BF16),
            pltpu.VMEM((4, 24, 16, ROWS), BF16),
            pltpu.VMEM((4, 24, 16, ROWS), BF16),
            pltpu.VMEM((2, 3, 128, ROWS), BF16),
            pltpu.VMEM((2, 4, 128, ROWS), BF16),
            dma, dma((2, 4)), dma((2, 4, 4)), dma((2, 4, 4)), dma((2, 4)), dma((2, 4)),
            dma, dma((16,)), dma((16,)), dma((2, 4)), dma((2, 4)),
        ],
        compiler_params=pltpu.CompilerParams(
            collective_id=0, has_side_effects=True, vmem_limit_bytes=56 * 1024 * 1024),
        cost_estimate=pl.CostEstimate(flops=8_000_000_000, bytes_accessed=12_000_000, transcendentals=0),
        name="spectral",
    )(pair_index, legendre.reshape(4, 4, 2, 5, 16, ROWS), grid, pcol, vertical)


def solution(mesh):
    placed = (P("lev", "lat", None), P(), P("lev", "lat", None), P())
    return jax.shard_map(
        body, mesh=mesh, in_specs=placed, out_specs=P("lev", "lat", None, None), check_vma=False
    )
```

```python
import math

import jax
import jax.numpy as jnp
from jax import lax
from jax.sharding import PartitionSpec as P
from jax.experimental import pallas as pl
from jax.experimental.pallas import tpu as pltpu

MESH = pl.DeviceIdType.MESH
F32 = jnp.float32
BF16 = jnp.bfloat16
NLON = 2560
NDEG = 1280
ROWS = 1280
HALF = ROWS // 2
LOW = 64
HIGH = NLON // 2 // LOW
DIST = (2, 1, 3, 0)


def iota(shape, dim):
    return lax.broadcasted_iota(jnp.int32, shape, dim)


def cos_sin(number):
    whole = jnp.floor(number * F32(1.0 / NLON) + F32(0.5))
    h = (number - whole * F32(NLON)) * F32(math.pi / NLON)
    h2 = h * h
    s = F32(-1.0 / 39916800.0)
    for c in (1.0 / 362880.0, -1.0 / 5040.0, 1.0 / 120.0, -1.0 / 6.0, 1.0):
        s = s * h2 + F32(c)
    s = s * h
    c_ = F32(1.0 / 479001600.0)
    for c in (-1.0 / 3628800.0, 1.0 / 40320.0, -1.0 / 720.0, 1.0 / 24.0, -0.5, 1.0):
        c_ = c_ * h2 + F32(c)
    return F32(1.0) - F32(2.0) * s * s, F32(2.0) * s * c_


def kernel(pair_ref, leg, grid_hbm, pair_v, vert, out,
           grid, even, odd, pairs, table, base_a, base_b, xs, xr, perm, zs, zr,
           wide, mixed, leg1, leg2, rs, rr, own,
           grid_sem, legl_sem, legs_sem, legr_sem, xs_sem, xr_sem, zl_sem, zs_sem, zr_sem, rs_sem, rr_sem):
    lat = lax.axis_index("lat")
    lev = lax.axis_index("lev")
    x, y = lat // 4, lat % 4

    def at_x(d):
        return (lax.rem(x + d, 4) * 4 + y, lev)

    def at_y(d):
        return (x * 4 + lax.rem(y + d, 4), lev)

    def at_z(e):
        return (lat, lax.rem(lev + e, 16))

    barrier = pltpu.get_barrier_semaphore()
    peers = [at_x(d) for d in (1, 2, 3)] + [at_y(d) for d in (1, 2, 3)] + [at_z(e) for e in range(1, 16)]
    for peer in peers:
        pl.semaphore_signal(barrier, inc=1, device_id=peer, device_id_type=MESH)

    grid_copy = pltpu.make_async_copy(grid_hbm, grid, grid_sem)
    grid_copy.start()

    local, remote = [], []
    for d in DIST:
        sy, sx = lax.rem(y + d, 4), lax.rem(x + d, 4)
        local.append((
            pltpu.make_async_copy(leg.at[x, sy, 0], leg1.at[sy, pl.ds(x * 5, 5)], legl_sem.at[0, d]),
            pltpu.make_async_copy(leg.at[sx, y, 1], leg2.at[sx, pl.ds(4 + y * 5, 5)], legl_sem.at[1, d]),
        ))
        group = []
        for e in (1, 3, 2):
            px, py = lax.rem(x + e, 4), lax.rem(y + e, 4)
            group.append(pltpu.make_async_remote_copy(
                src_ref=leg.at[px, sy, 0], dst_ref=leg1.at[sy, pl.ds(x * 5, 5)],
                send_sem=legs_sem.at[0, d, e], recv_sem=legr_sem.at[0, d, e],
                device_id=at_x(e), device_id_type=MESH))
            group.append(pltpu.make_async_remote_copy(
                src_ref=leg.at[sx, py, 1], dst_ref=leg2.at[sx, pl.ds(4 + y * 5, 5)],
                send_sem=legs_sem.at[1, d, e], recv_sem=legr_sem.at[1, d, e],
                device_id=at_y(e), device_id_type=MESH))
        remote.append(group)

    pairs[0:4] = pair_v[...]
    pairs[4:8] = jnp.zeros((4, 128), jnp.int32)

    def columns(g, d):
        t = iota((8, 128), 1)
        s = (t >> 1) & 3
        there = (lev + (4 + 8 * g) + ((t >> 3) & 7)) & 15
        dx, dy = lax.rem(x + d, 4), lax.rem(y + d, 4)
        index = there * 32 + jnp.where(t < 64, dx * 8 + s * 2, s * 8 + dy * 2 + 1)
        got = jnp.take_along_axis(pairs[...], index & 127, axis=1)
        mine = iota((8, 128), 0) == (index >> 7)
        return jnp.sum(jnp.where(mine, got, 0).astype(F32), axis=0, keepdims=True)

    def make_table(buf, g, q):
        for n in range(2):
            d = DIST[2 * q + n]
            p = columns(g, d)
            high = (iota((24, 128), 0) * (2 * LOW)).astype(F32)
            cos, sin = cos_sin(high * p)
            imag = (iota((24, 128), 1) & 1) == 1
            factor = F32(1.0 / math.sqrt(NLON))
            base_a[buf, n] = jnp.where(imag, -sin, cos) * factor
            base_b[buf, n] = jnp.where(imag, -cos, -sin) * factor
            for o in range(2):
                low = (iota((LOW, 128), 0) * 2 + o).astype(F32)
                cos, sin = cos_sin(low * p)
                for i in range(HIGH):
                    block = base_a[buf, n, i:i + 1] * cos + base_b[buf, n, i:i + 1] * sin
                    table[buf, o, i * LOW:(i + 1) * LOW, n * 128:(n + 1) * 128] = block.astype(BF16)

    row, col = iota((256, 256), 0), iota((256, 256), 1)
    parted = (row == 2 * (col & 127) + (col >> 7)).astype(BF16)
    row, col = iota((128, 128), 0), iota((128, 128), 1)
    want = ((row >> 3) & 1) * 64 + (row >> 4) * 8 + (row & 7)
    minus = (((row >> 3) & 1) == 1) & ((row & 1) == 1)
    perm[...] = jnp.where(col == want, jnp.where(minus, F32(-1.0), F32(1.0)), F32(0.0)).astype(BF16)

    make_table(0, 0, 0)
    grid_copy.wait()
    for b in range(NLON // 256):
        halves = jnp.dot(grid[:, :, b * 256:(b + 1) * 256].reshape(320, 256), parted,
                         preferred_element_type=F32).astype(BF16)
        even[:, b * 128:(b + 1) * 128] = halves[:, 0:128]
        odd[:, b * 128:(b + 1) * 128] = halves[:, 128:256]

    pl.semaphore_wait(barrier, len(peers))
    for copy in remote[0][0:4]:
        copy.start()
    for pair in local:
        for copy in pair:
            copy.start()

    lane_low = iota((320, 128), 1) < 64
    x_copies = []
    for g in range(2):
        for q in range(2):
            buf = q
            if g + q > 0:
                make_table(buf, g, q)
            a = jnp.dot(even[...], table[buf, 0], preferred_element_type=F32)
            b = jnp.dot(odd[...], table[buf, 1], preferred_element_type=F32)
            for n in range(2):
                d = DIST[2 * q + n]
                plus = (a + b)[:, n * 128:(n + 1) * 128]
                less = (a - b)[:, n * 128:(n + 1) * 128]
                for h in range(2):
                    if h == 0:
                        part = jnp.where(lane_low, plus, pltpu.roll(less, 64, 1))
                    else:
                        part = jnp.where(lane_low, pltpu.roll(plus, 64, 1), less)
                    part = part.astype(BF16).reshape(4, 80, 128)
                    here = x if h == 0 else 4 + y
                    if d == 0:
                        xr[g, :, here] = part
                        continue
                    xs[g, d - 1, h] = part
                    copy = pltpu.make_async_remote_copy(
                        src_ref=xs.at[g, d - 1, h], dst_ref=xr.at[g, :, here],
                        send_sem=xs_sem.at[g, h, d], recv_sem=xr_sem.at[g, h, d],
                        device_id=at_x(d) if h == 0 else at_y(d), device_id_type=MESH)
                    copy.start()
                    x_copies.append((g, copy))
        if g == 0:
            for copy in remote[0][4:]:
                copy.start()
    for copy in remote[1]:
        copy.start()

    z_copies = []
    for g in range(2):
        for gg, copy in x_copies:
            if gg == g:
                copy.wait()
        for l in range(4):
            turned = lax.dot_general(perm[...], xr[g, l].reshape(640, 128), (((1,), (1,)), ((), ())),
                                     preferred_element_type=F32).astype(BF16)
            zs[g, :, l] = turned.reshape(8, 16, 640)
        for i in ((4, 3, 5, 2, 6, 1, 7, 0), (0, 7, 1, 6, 2, 5, 3))[g]:
            e = (4 + 8 * g + i) % 16
            copy = pltpu.make_async_remote_copy(
                src_ref=zs.at[g, i], dst_ref=zr.at[lev],
                send_sem=zs_sem.at[e], recv_sem=zr_sem.at[e],
                device_id=at_z(e), device_id_type=MESH)
            copy.start()
            z_copies.append(copy)
        for copy in remote[2 + g]:
            copy.start()
    z_own = pltpu.make_async_copy(zs.at[1, 4], zr.at[lev], zl_sem)
    z_own.start()

    leg1[:, 20:24] = jnp.zeros((4, 4, 16, ROWS), BF16)
    leg2[:, 0:4] = jnp.zeros((4, 4, 16, ROWS), BF16)
    level_of = ((iota((64, 1024), 1) >> 4) == iota((64, 1024), 0)).astype(BF16)
    spread = jnp.dot(vert[...], level_of, preferred_element_type=F32)
    inner = iota((64, 1024), 1) & 15
    for s in range(4):
        for u in range(2):
            for c in range(2):
                i = s * 4 + u * 2 + c
                wide[i * 64:(i + 1) * 64, :] = jnp.where(inner == u * 8 + s * 2 + c, spread, F32(0.0)).astype(BF16)

    z_own.wait()
    for copy in z_copies:
        copy.wait()
    mixed[...] = jnp.dot(wide[...], zr[...].reshape(1024, 640), preferred_element_type=F32).astype(BF16)

    def summed(h, d, part):
        s = lax.rem((y if h == 0 else x) + d, 4)
        legs = leg1 if h == 0 else leg2
        lanes = slice(0, 384) if h == 0 else slice(256, 640)
        table_half = legs[s, :, :, part * HALF:(part + 1) * HALF].reshape(384, HALF)
        if part == 0:
            g = mixed[pl.ds(pl.multiple_of(s * 256, 256), 128), lanes]
            return jnp.dot(g, table_half, preferred_element_type=F32)
        slot = lev * 32 + ((x * 4 + s) * 2 if h == 0 else (s * 4 + y) * 2 + 1)
        g = mixed[pl.ds(pl.multiple_of(s * 256, 256), 256), lanes]
        both = jnp.dot(g, table_half, preferred_element_type=F32)
        first = iota((128, HALF), 1) + HALF < NDEG - pair_ref[slot]
        return jnp.where(first, both[0:128], both[128:256])

    def arrived(n):
        for copy in local[n]:
            copy.wait()
        for copy in remote[n]:
            copy.wait()

    out_copies = {}

    def send(h, k, part, value):
        rs[h, k, part] = value.astype(BF16)
        step = (1, 1, 3)[k] if k > 0 else (1, 3)[part]
        copy = pltpu.make_async_remote_copy(
            src_ref=rs.at[h, k, part], dst_ref=rr.at[h, k, part],
            send_sem=rs_sem.at[h, k, part], recv_sem=rr_sem.at[h, k, part],
            device_id=at_y(step) if h == 0 else at_x(step), device_id_type=MESH)
        copy.start()
        out_copies[h, k, part] = copy

    arrived(0)
    for h in range(2):
        for part in range(2):
            send(h, 0, part, summed(h, 2, part))
    arrived(1)
    for h in range(2):
        send(h, 1, 1, summed(h, 1, 1))
    arrived(2)
    for h in range(2):
        send(h, 2, 0, summed(h, 3, 0))
    for k, part in ((1, 0), (2, 1)):
        for h in range(2):
            value = summed(h, 1 if k == 1 else 3, part)
            out_copies[h, 0, part].wait()
            send(h, k, part, value + rr[h, 0, part].astype(F32))
    arrived(3)
    for h in range(2):
        for part in range(2):
            own[h, part] = summed(h, 0, part)
    for part in range(2):
        for h in range(2):
            for k in (1, 2):
                out_copies[h, k, part].wait()
            for r in range(0, HALF, 128):
                total = own[h, part, :, r:r + 128]
                for k in (1, 2):
                    total = total + rr[h, k, part, :, r:r + 128].astype(F32)
                out[0, h, part * HALF + r:part * HALF + r + 128, :] = total.T.astype(BF16)


def body(grid, pair_index, legendre, vertical):
    vmem = pl.BlockSpec(memory_space=pltpu.VMEM)
    hbm = pl.BlockSpec(memory_space=pl.ANY)
    dma = pltpu.SemaphoreType.DMA
    return pl.pallas_call(
        kernel,
        out_shape=jax.ShapeDtypeStruct((1, 2, ROWS, 128), BF16),
        in_specs=[pl.BlockSpec(memory_space=pltpu.SMEM), hbm, hbm, vmem, vmem],
        out_specs=vmem,
        scratch_shapes=[
            pltpu.VMEM((4, 80, NLON), BF16),
            pltpu.VMEM((320, NLON // 2), BF16),
            pltpu.VMEM((320, NLON // 2), BF16),
            pltpu.VMEM((8, 128), jnp.int32),
            pltpu.VMEM((2, 2, NLON // 2, 256), BF16),
            pltpu.VMEM((2, 2, 24, 128), F32),
            pltpu.VMEM((2, 2, 24, 128), F32),
            pltpu.VMEM((2, 3, 2, 4, 80, 128), BF16),
            pltpu.VMEM((2, 4, 8, 80, 128), BF16),
            pltpu.VMEM((128, 128), BF16),
            pltpu.VMEM((2, 8, 4, 16, 640), BF16),
            pltpu.VMEM((16, 4, 16, 640), BF16),
            pltpu.VMEM((1024, 1024), BF16),
            pltpu.VMEM((1024, 640), BF16),
            pltpu.VMEM((4, 24, 16, ROWS), BF16),
            pltpu.VMEM((4, 24, 16, ROWS), BF16),
            pltpu.VMEM((2, 3, 2, 128, HALF), BF16),
            pltpu.VMEM((2, 3, 2, 128, HALF), BF16),
            pltpu.VMEM((2, 2, 128, HALF), F32),
            dma, dma((2, 4)), dma((2, 4, 4)), dma((2, 4, 4)), dma((2, 2, 4)), dma((2, 2, 4)),
            dma, dma((16,)), dma((16,)), dma((2, 3, 2)), dma((2, 3, 2)),
        ],
        compiler_params=pltpu.CompilerParams(
            collective_id=0, has_side_effects=True, vmem_limit_bytes=56 * 1024 * 1024),
        cost_estimate=pl.CostEstimate(flops=8_000_000_000, bytes_accessed=12_000_000, transcendentals=0),
        name="spectral",
    )(pair_index, legendre.reshape(4, 4, 2, 5, 16, ROWS), grid, pair_index.reshape(4, 128), vertical)


def solution(mesh):
    placed = (P("lev", "lat", None), P(), P("lev", "lat", None), P())
    return jax.shard_map(
        body, mesh=mesh, in_specs=placed, out_specs=P("lev", "lat", None, None), check_vma=False
    )
```

```python
import math

import jax
import jax.numpy as jnp
from jax import lax
from jax.sharding import PartitionSpec as P
from jax.experimental import pallas as pl
from jax.experimental.pallas import tpu as pltpu

MESH = pl.DeviceIdType.MESH
F32 = jnp.float32
BF16 = jnp.bfloat16
NLON = 2560
NDEG = 1280
ROWS = 1280
HALF = ROWS // 2
LOW = 64
HIGH = NLON // 2 // LOW
DIST = (2, 1, 3, 0)
VMEM_MIB = 52


def iota(shape, dim):
    return lax.broadcasted_iota(jnp.int32, shape, dim)


def cos_sin(number):
    whole = jnp.floor(number * F32(1.0 / NLON) + F32(0.5))
    h = (number - whole * F32(NLON)) * F32(math.pi / NLON)
    h2 = h * h
    s = F32(-1.0 / 39916800.0)
    for c in (1.0 / 362880.0, -1.0 / 5040.0, 1.0 / 120.0, -1.0 / 6.0, 1.0):
        s = s * h2 + F32(c)
    s = s * h
    c_ = F32(1.0 / 479001600.0)
    for c in (-1.0 / 3628800.0, 1.0 / 40320.0, -1.0 / 720.0, 1.0 / 24.0, -0.5, 1.0):
        c_ = c_ * h2 + F32(c)
    return F32(1.0) - F32(2.0) * s * s, F32(2.0) * s * c_


def kernel(leg, grid_hbm, pair_hbm, vert_hbm, out,
           grid, vert, even, odd, pairs, table, base_a, base_b, xs, xr, perm, zs, zr,
           wide, half_mixed, mixed, leg1, leg2, rs, rr, own,
           in_sem, legl_sem, legs_sem, legr_sem, xs_sem, xr_sem, zl_sem, zs_sem, zr_sem, rs_sem, rr_sem):
    lat = lax.axis_index("lat")
    lev = lax.axis_index("lev")
    x, y = lat // 4, lat % 4

    def at_x(d):
        return (lax.rem(x + d, 4) * 4 + y, lev)

    def at_y(d):
        return (x * 4 + lax.rem(y + d, 4), lev)

    def at_z(e):
        return (lat, lax.rem(lev + e, 16))

    barrier = pltpu.get_barrier_semaphore()
    peers = [at_x(d) for d in (1, 2, 3)] + [at_y(d) for d in (1, 2, 3)] + [at_z(e) for e in range(1, 16)]
    for peer in peers:
        pl.semaphore_signal(barrier, inc=1, device_id=peer, device_id_type=MESH)

    pair_copy = pltpu.make_async_copy(pair_hbm, pairs.at[pl.ds(0, 4)], in_sem.at[0])
    grid_copy = pltpu.make_async_copy(grid_hbm, grid, in_sem.at[1])
    vert_copy = pltpu.make_async_copy(vert_hbm, vert, in_sem.at[2])
    pair_copy.start()
    grid_copy.start()
    vert_copy.start()

    local, remote = [], []
    for d in DIST:
        sy, sx = lax.rem(y + d, 4), lax.rem(x + d, 4)
        local.append((
            pltpu.make_async_copy(leg.at[x, sy, 0], leg1.at[sy, pl.ds(x * 5, 5)], legl_sem.at[0, d]),
            pltpu.make_async_copy(leg.at[sx, y, 1], leg2.at[sx, pl.ds(4 + y * 5, 5)], legl_sem.at[1, d]),
        ))
        group = []
        for e in (1, 3, 2):
            px, py = lax.rem(x + e, 4), lax.rem(y + e, 4)
            group.append(pltpu.make_async_remote_copy(
                src_ref=leg.at[px, sy, 0], dst_ref=leg1.at[sy, pl.ds(x * 5, 5)],
                send_sem=legs_sem.at[0, d, e], recv_sem=legr_sem.at[0, d, e],
                device_id=at_x(e), device_id_type=MESH))
            group.append(pltpu.make_async_remote_copy(
                src_ref=leg.at[sx, py, 1], dst_ref=leg2.at[sx, pl.ds(4 + y * 5, 5)],
                send_sem=legs_sem.at[1, d, e], recv_sem=legr_sem.at[1, d, e],
                device_id=at_y(e), device_id_type=MESH))
        remote.append(group)

    pl.semaphore_wait(barrier, len(peers))
    for copy in remote[0][0:4]:
        copy.start()


    def columns(g, d):
        t = iota((8, 128), 1)
        s = (t >> 1) & 3
        there = (lev + (4 + 8 * g) + ((t >> 3) & 7)) & 15
        dx, dy = lax.rem(x + d, 4), lax.rem(y + d, 4)
        index = there * 32 + jnp.where(t < 64, dx * 8 + s * 2, s * 8 + dy * 2 + 1)
        got = jnp.take_along_axis(pairs[...], index & 127, axis=1)
        mine = iota((8, 128), 0) == (index >> 7)
        return jnp.sum(jnp.where(mine, got, 0).astype(F32), axis=0, keepdims=True)

    def make_table(buf, g, q):
        for n in range(2):
            d = DIST[2 * q + n]
            p = columns(g, d)
            high = (iota((24, 128), 0) * (2 * LOW)).astype(F32)
            cos, sin = cos_sin(high * p)
            imag = (iota((24, 128), 1) & 1) == 1
            factor = F32(1.0 / math.sqrt(NLON))
            base_a[buf, n] = jnp.where(imag, -sin, cos) * factor
            base_b[buf, n] = jnp.where(imag, -cos, -sin) * factor
            for o in range(2):
                low = (iota((LOW, 128), 0) * 2 + o).astype(F32)
                cos, sin = cos_sin(low * p)
                for i in range(HIGH):
                    block = base_a[buf, n, i:i + 1] * cos + base_b[buf, n, i:i + 1] * sin
                    table[buf, o, i * LOW:(i + 1) * LOW, n * 128:(n + 1) * 128] = block.astype(BF16)

    row, col = iota((256, 256), 0), iota((256, 256), 1)
    parted = (row == 2 * (col & 127) + (col >> 7)).astype(BF16)
    row, col = iota((128, 128), 0), iota((128, 128), 1)
    want = ((row >> 3) & 1) * 64 + (row >> 4) * 8 + (row & 7)
    minus = (((row >> 3) & 1) == 1) & ((row & 1) == 1)
    perm[...] = jnp.where(col == want, jnp.where(minus, F32(-1.0), F32(1.0)), F32(0.0)).astype(BF16)

    pairs[4:8] = jnp.zeros((4, 128), jnp.int32)
    pair_copy.wait()
    make_table(0, 0, 0)
    grid_copy.wait()
    for b in range(NLON // 256):
        halves = jnp.dot(grid[:, :, b * 256:(b + 1) * 256].reshape(320, 256), parted,
                         preferred_element_type=F32).astype(BF16)
        even[:, b * 128:(b + 1) * 128] = halves[:, 0:128]
        odd[:, b * 128:(b + 1) * 128] = halves[:, 128:256]

    lane_low = iota((320, 128), 1) < 64
    x_copies = []
    for g in range(2):
        for q in range(2):
            buf = q
            if g + q > 0:
                make_table(buf, g, q)
            a = jnp.dot(even[...], table[buf, 0], preferred_element_type=F32)
            b = jnp.dot(odd[...], table[buf, 1], preferred_element_type=F32)
            for n in range(2):
                d = DIST[2 * q + n]
                plus = (a + b)[:, n * 128:(n + 1) * 128]
                less = (a - b)[:, n * 128:(n + 1) * 128]
                for h in range(2):
                    if h == 0:
                        part = jnp.where(lane_low, plus, pltpu.roll(less, 64, 1))
                    else:
                        part = jnp.where(lane_low, pltpu.roll(plus, 64, 1), less)
                    part = part.astype(BF16).reshape(4, 80, 128)
                    here = x if h == 0 else 4 + y
                    if d == 0:
                        xr[g, :, here] = part
                        continue
                    xs[g, d - 1, h] = part
                    copy = pltpu.make_async_remote_copy(
                        src_ref=xs.at[g, d - 1, h], dst_ref=xr.at[g, :, here],
                        send_sem=xs_sem.at[g, h, d], recv_sem=xr_sem.at[g, h, d],
                        device_id=at_x(d) if h == 0 else at_y(d), device_id_type=MESH)
                    copy.start()
                    x_copies.append((g, copy))
        if g == 0:
            for copy in remote[0][4:]:
                copy.start()
            for pair in local:
                for copy in pair:
                    copy.start()
    for copy in remote[1]:
        copy.start()

    z_copies = []
    for g in range(2):
        for gg, copy in x_copies:
            if gg == g:
                copy.wait()
        for l in range(4):
            turned = lax.dot_general(perm[...], xr[g, l].reshape(640, 128), (((1,), (1,)), ((), ())),
                                     preferred_element_type=F32).astype(BF16)
            zs[g, :, l] = turned.reshape(8, 16, 640)
        for i in ((4, 3, 5, 2, 6, 1, 7, 0), (0, 7, 1, 6, 2, 5, 3))[g]:
            e = (4 + 8 * g + i) % 16
            copy = pltpu.make_async_remote_copy(
                src_ref=zs.at[g, i], dst_ref=zr.at[g, i],
                send_sem=zs_sem.at[e], recv_sem=zr_sem.at[e],
                device_id=at_z(e), device_id_type=MESH)
            copy.start()
            z_copies.append((g, copy))
        for copy in remote[2 + g]:
            copy.start()
    z_own = pltpu.make_async_copy(zs.at[1, 4], zr.at[1, 4], zl_sem)
    z_own.start()

    leg1[:, 20:24] = jnp.zeros((4, 4, 16, ROWS), BF16)
    leg2[:, 0:4] = jnp.zeros((4, 4, 16, ROWS), BF16)
    vert_copy.wait()
    col = iota((64, 1024), 1)
    level = ((lev + 12 - (col >> 6)) & 15) * 4 + ((col >> 4) & 3)
    level_of = (level == iota((64, 1024), 0)).astype(BF16)
    spread = jnp.dot(vert[...], level_of, preferred_element_type=F32)
    inner = iota((64, 1024), 1) & 15
    for s in range(4):
        for u in range(2):
            for c in range(2):
                i = s * 4 + u * 2 + c
                wide[i * 64:(i + 1) * 64, :] = jnp.where(inner == u * 8 + s * 2 + c, spread, F32(0.0)).astype(BF16)

    for g, copy in z_copies:
        if g == 0:
            copy.wait()
    half_mixed[...] = jnp.dot(wide[:, 0:512], zr[0].reshape(512, 640), preferred_element_type=F32)
    z_own.wait()
    for g, copy in z_copies:
        if g == 1:
            copy.wait()
    mixed[...] = (half_mixed[...] + jnp.dot(wide[:, 512:1024], zr[1].reshape(512, 640),
                                            preferred_element_type=F32)).astype(BF16)

    def summed(h, d, part):
        s = lax.rem((y if h == 0 else x) + d, 4)
        legs = leg1 if h == 0 else leg2
        lanes = slice(0, 384) if h == 0 else slice(256, 640)
        table_half = legs[s, :, :, part * HALF:(part + 1) * HALF].reshape(384, HALF)
        if part == 0:
            g = mixed[pl.ds(pl.multiple_of(s * 256, 256), 128), lanes]
            return jnp.dot(g, table_half, preferred_element_type=F32)
        slot = lev * 32 + ((x * 4 + s) * 2 if h == 0 else (s * 4 + y) * 2 + 1)
        g = mixed[pl.ds(pl.multiple_of(s * 256, 256), 256), lanes]
        both = jnp.dot(g, table_half, preferred_element_type=F32)
        mine = iota((8, 128), 0) * 128 + iota((8, 128), 1) == slot
        p = jnp.sum(jnp.where(mine, pairs[...], 0).astype(F32), keepdims=True).astype(jnp.int32)
        first = iota((128, HALF), 1) + HALF < NDEG - p
        return jnp.where(first, both[0:128], both[128:256])

    def arrived(n):
        for copy in local[n]:
            copy.wait()
        for copy in remote[n]:
            copy.wait()

    out_copies = {}

    def send(h, k, part, value):
        rs[h, k, part] = value.astype(BF16)
        step = (1, 1, 3)[k] if k > 0 else (1, 3)[part]
        copy = pltpu.make_async_remote_copy(
            src_ref=rs.at[h, k, part], dst_ref=rr.at[h, k, part],
            send_sem=rs_sem.at[h, k, part], recv_sem=rr_sem.at[h, k, part],
            device_id=at_y(step) if h == 0 else at_x(step), device_id_type=MESH)
        copy.start()
        out_copies[h, k, part] = copy

    arrived(0)
    for h in range(2):
        for part in range(2):
            send(h, 0, part, summed(h, 2, part))
    arrived(1)
    for h in range(2):
        send(h, 1, 1, summed(h, 1, 1))
    arrived(2)
    for h in range(2):
        send(h, 2, 0, summed(h, 3, 0))
    for k, part in ((1, 0), (2, 1)):
        for h in range(2):
            value = summed(h, 1 if k == 1 else 3, part)
            out_copies[h, 0, part].wait()
            send(h, k, part, value + rr[h, 0, part].astype(F32))
    arrived(3)
    for h in range(2):
        for part in range(2):
            own[h, part] = summed(h, 0, part)
    for part in range(2):
        for h in range(2):
            for k in (1, 2):
                out_copies[h, k, part].wait()
            for r in range(0, HALF, 128):
                total = own[h, part, :, r:r + 128]
                for k in (1, 2):
                    total = total + rr[h, k, part, :, r:r + 128].astype(F32)
                out[0, h, part * HALF + r:part * HALF + r + 128, :] = total.T.astype(BF16)


def body(grid, pair_index, legendre, vertical):
    vmem = pl.BlockSpec(memory_space=pltpu.VMEM)
    hbm = pl.BlockSpec(memory_space=pl.ANY)
    dma = pltpu.SemaphoreType.DMA
    return pl.pallas_call(
        kernel,
        out_shape=jax.ShapeDtypeStruct((1, 2, ROWS, 128), BF16),
        in_specs=[hbm, hbm, hbm, hbm],
        out_specs=vmem,
        scratch_shapes=[
            pltpu.VMEM((4, 80, NLON), BF16),
            pltpu.VMEM((64, 64), BF16),
            pltpu.VMEM((320, NLON // 2), BF16),
            pltpu.VMEM((320, NLON // 2), BF16),
            pltpu.VMEM((8, 128), jnp.int32),
            pltpu.VMEM((2, 2, NLON // 2, 256), BF16),
            pltpu.VMEM((2, 2, 24, 128), F32),
            pltpu.VMEM((2, 2, 24, 128), F32),
            pltpu.VMEM((2, 3, 2, 4, 80, 128), BF16),
            pltpu.VMEM((2, 4, 8, 80, 128), BF16),
            pltpu.VMEM((128, 128), BF16),
            pltpu.VMEM((2, 8, 4, 16, 640), BF16),
            pltpu.VMEM((2, 8, 4, 16, 640), BF16),
            pltpu.VMEM((1024, 1024), BF16),
            pltpu.VMEM((1024, 640), F32),
            pltpu.VMEM((1024, 640), BF16),
            pltpu.VMEM((4, 24, 16, ROWS), BF16),
            pltpu.VMEM((4, 24, 16, ROWS), BF16),
            pltpu.VMEM((2, 3, 2, 128, HALF), BF16),
            pltpu.VMEM((2, 3, 2, 128, HALF), BF16),
            pltpu.VMEM((2, 2, 128, HALF), F32),
            dma((3,)), dma((2, 4)), dma((2, 4, 4)), dma((2, 4, 4)), dma((2, 2, 4)), dma((2, 2, 4)),
            dma, dma((16,)), dma((16,)), dma((2, 3, 2)), dma((2, 3, 2)),
        ],
        compiler_params=pltpu.CompilerParams(
            collective_id=0, has_side_effects=True, vmem_limit_bytes=VMEM_MIB * 1024 * 1024),
        cost_estimate=pl.CostEstimate(flops=8_000_000_000, bytes_accessed=12_000_000, transcendentals=0),
        name="spectral",
    )(legendre.reshape(4, 4, 2, 5, 16, ROWS), grid, pair_index.reshape(4, 128), vertical)


def solution(mesh):
    placed = (P("lev", "lat", None), P(), P("lev", "lat", None), P())
    return jax.shard_map(
        body, mesh=mesh, in_specs=placed, out_specs=P("lev", "lat", None, None), check_vma=False
    )
```

```python
import math

import jax
import jax.numpy as jnp
from jax import lax
from jax.sharding import PartitionSpec as P
from jax.experimental import pallas as pl
from jax.experimental.pallas import tpu as pltpu

MESH = pl.DeviceIdType.MESH
F32 = jnp.float32
BF16 = jnp.bfloat16
NLON = 2560
NDEG = 1280
ROWS = 1280
HALF = ROWS // 2
LOW = 64
HIGH = NLON // 2 // LOW
BLOCKS = ((1, 2), (2, 3), (0, 1), (3, 0))
CHUNKS = (((0, 2), (0, 3), (0, 4), (0, 5)), ((0, 0), (0, 1), (0, 6), (0, 7)),
          ((1, 0), (1, 1), (1, 6), (1, 7)), ((1, 2), (1, 3), (1, 4), (1, 5)))
VMEM_MIB = 52


def iota(shape, dim):
    return lax.broadcasted_iota(jnp.int32, shape, dim)


def cos_sin(number):
    whole = jnp.floor(number * F32(1.0 / NLON) + F32(0.5))
    h = (number - whole * F32(NLON)) * F32(math.pi / NLON)
    h2 = h * h
    s = F32(-1.0 / 39916800.0)
    for c in (1.0 / 362880.0, -1.0 / 5040.0, 1.0 / 120.0, -1.0 / 6.0, 1.0):
        s = s * h2 + F32(c)
    s = s * h
    c_ = F32(1.0 / 479001600.0)
    for c in (-1.0 / 3628800.0, 1.0 / 40320.0, -1.0 / 720.0, 1.0 / 24.0, -0.5, 1.0):
        c_ = c_ * h2 + F32(c)
    return F32(1.0) - F32(2.0) * s * s, F32(2.0) * s * c_


def kernel(leg, grid_hbm, pair_hbm, vert_hbm, out,
           grid, vert, even, odd, pairs, limit, table, base_a, base_b, xs, xr, perm, spread, zs, zr,
           mixed, legs, t1, r1, rs, rr, keep, own, total, wide,
           in_sem, legl_sem, legs_sem, legr_sem, xs_sem, xr_sem, zs_sem, zr_sem,
           ts_sem, tr_sem, rs_sem, rr_sem):
    lat = lax.axis_index("lat")
    lev = lax.axis_index("lev")
    x, y = lat // 4, lat % 4

    def at(axis, d):
        if axis == 0:
            return (lax.rem(x + d, 4) * 4 + y, lev)
        return (x * 4 + lax.rem(y + d, 4), lev)

    def at_z(e):
        return (lat, lax.rem(lev + e, 16))

    barrier = pltpu.get_barrier_semaphore()
    peers = [at(axis, d) for axis in (0, 1) for d in (1, 3)] + [at_z(e) for e in range(1, 16)]
    for peer in peers:
        pl.semaphore_signal(barrier, inc=1, device_id=peer, device_id_type=MESH)

    pair_copy = pltpu.make_async_copy(pair_hbm, pairs.at[pl.ds(0, 4)], in_sem.at[0])
    grid_copy = pltpu.make_async_copy(grid_hbm, grid, in_sem.at[1])
    vert_copy = pltpu.make_async_copy(vert_hbm, vert, in_sem.at[2])
    pair_copy.start()
    grid_copy.start()
    vert_copy.start()

    def source(h, d, s):
        if h == 0:
            return leg.at[lax.rem(x + d, 4), s, 0]
        return leg.at[s, lax.rem(y + d, 4), 1]

    local, remote = [], []
    for s in range(4):
        for h in range(2):
            for n in range(2):
                to = BLOCKS[n][s % 2]
                first = (2 * h + n) * 2
                remote.append(pltpu.make_async_remote_copy(
                    src_ref=source(h, to, s), dst_ref=legs.at[h, n, s, pl.ds(first + 5 * n, 5)],
                    send_sem=legs_sem.at[h, n, s], recv_sem=legr_sem.at[h, n, s],
                    device_id=at(h, 1 if n == 0 else 3), device_id_type=MESH))
                to = BLOCKS[2 + n][s % 2]
                local.append(pltpu.make_async_copy(
                    source(h, to, s), legs.at[h, n, s, pl.ds(first + 5 - 5 * n, 5)], legl_sem.at[h, n, s]))

    pl.semaphore_wait(barrier, len(peers))
    for copy in remote[0:4]:
        copy.start()

    def columns(g, n):
        t = iota((8, 128), 1)
        s = (t >> 1) & 3
        there = (lev + (12 + 8 * g) + ((t >> 3) & 7)) & 15
        ahead = jnp.where((s & 1) == 1, BLOCKS[n][1], BLOCKS[n][0])
        index = there * 32 + jnp.where(t < 64, ((x + ahead) & 3) * 8 + s * 2, s * 8 + ((y + ahead) & 3) * 2 + 1)
        got = jnp.take_along_axis(pairs[...], index & 127, axis=1)
        mine = iota((8, 128), 0) == (index >> 7)
        return jnp.sum(jnp.where(mine, got, 0).astype(F32), axis=0, keepdims=True)

    def make_table(buf, g, q):
        for n in range(2):
            p = columns(g, 2 * q + n)
            high = (iota((24, 128), 0) * (2 * LOW)).astype(F32)
            cos, sin = cos_sin(high * p)
            imag = (iota((24, 128), 1) & 1) == 1
            factor = F32(1.0 / math.sqrt(NLON))
            base_a[buf, n] = jnp.where(imag, -sin, cos) * factor
            base_b[buf, n] = jnp.where(imag, -cos, -sin) * factor
            for o in range(2):
                low = (iota((LOW, 128), 0) * 2 + o).astype(F32)
                cos, sin = cos_sin(low * p)
                for i in range(HIGH):
                    block = base_a[buf, n, i:i + 1] * cos + base_b[buf, n, i:i + 1] * sin
                    table[buf, o, i * LOW:(i + 1) * LOW, n * 128:(n + 1) * 128] = block.astype(BF16)

    row, col = iota((256, 256), 0), iota((256, 256), 1)
    parted = (row == 2 * (col & 127) + (col >> 7)).astype(BF16)
    row, col = iota((128, 128), 0), iota((128, 128), 1)
    want = ((row >> 3) & 1) * 64 + (row >> 4) * 8 + (row & 7)
    minus = (((row >> 3) & 1) == 1) & ((row & 1) == 1)
    perm[...] = jnp.where(col == want, jnp.where(minus, F32(-1.0), F32(1.0)), F32(0.0)).astype(BF16)

    pairs[4:8] = jnp.zeros((4, 128), jnp.int32)
    pair_copy.wait()
    make_table(0, 0, 0)
    grid_copy.wait()
    for b in range(NLON // 256):
        halves = jnp.dot(grid[:, :, b * 256:(b + 1) * 256].reshape(320, 256), parted,
                         preferred_element_type=F32).astype(BF16)
        even[:, b * 128:(b + 1) * 128] = halves[:, 0:128]
        odd[:, b * 128:(b + 1) * 128] = halves[:, 128:256]

    lane_low = iota((320, 128), 1) < 64
    x_copies = []
    for g in range(2):
        for q in range(2):
            if g + q > 0:
                make_table(q, g, q)
            a = jnp.dot(even[...], table[q, 0], preferred_element_type=F32)
            b = jnp.dot(odd[...], table[q, 1], preferred_element_type=F32)
            for n in range(2):
                plus = (a + b)[:, n * 128:(n + 1) * 128]
                less = (a - b)[:, n * 128:(n + 1) * 128]
                for h in range(2):
                    if h == 0:
                        part = jnp.where(lane_low, plus, pltpu.roll(less, 64, 1))
                    else:
                        part = jnp.where(lane_low, pltpu.roll(plus, 64, 1), less)
                    part = part.astype(BF16).reshape(4, 80, 128)
                    if q == 1:
                        xr[g, :, h * 4 + 1 + n] = part
                        continue
                    xs[g, n, h] = part
                    copy = pltpu.make_async_remote_copy(
                        src_ref=xs.at[g, n, h], dst_ref=xr.at[g, :, h * 4 + 3 * n],
                        send_sem=xs_sem.at[g, n, h], recv_sem=xr_sem.at[g, n, h],
                        device_id=at(h, 1 if n == 0 else 3), device_id_type=MESH)
                    copy.start()
                    x_copies.append((g, copy))
        for copy in remote[4:8] if g == 0 else remote[8:16]:
            copy.start()
        if g == 0:
            for copy in local:
                copy.start()

    z_copies = {}
    for g in range(2):
        for gg, copy in x_copies:
            if gg == g:
                copy.wait()
        for l in range(4):
            turned = lax.dot_general(perm[...], xr[g, l].reshape(640, 128), (((1,), (1,)), ((), ())),
                                     preferred_element_type=F32).astype(BF16)
            zs[g, :, l] = turned.reshape(8, 16, 640)
            if g == 0:
                zr[0, 2, l] = turned[64:80]
        for q in (2 * g, 2 * g + 1):
            for k, (_, i) in enumerate(CHUNKS[q]):
                e = (12 + 8 * g + i) % 16
                if e == 0:
                    continue
                copy = pltpu.make_async_remote_copy(
                    src_ref=zs.at[g, i], dst_ref=zr.at[q, k],
                    send_sem=zs_sem.at[q, k], recv_sem=zr_sem.at[q, k],
                    device_id=at_z(e), device_id_type=MESH)
                copy.start()
                z_copies[q, k] = copy

    for h in range(2):
        for n in range(2):
            first = (2 * h + n) * 2
            if first > 0:
                legs[h, n, :, 0:first] = jnp.zeros((4, first, 16, ROWS), BF16)
            if first < 6:
                legs[h, n, :, first + 10:16] = jnp.zeros((4, 6 - first, 16, ROWS), BF16)
    row, col = iota((256, 256), 0), iota((256, 256), 1)
    want = (row & 15) * 16 + ((row >> 5) & 1) * 8 + (row >> 6) * 2 + ((row >> 4) & 1)
    spread[...] = (col == want).astype(BF16)
    for h in range(2):
        for role in range(2):
            for s in range(4):
                d = 0 if role == 1 else (1 if s % 2 == 1 else 3)
                if h == 0:
                    slot = lev * 32 + lax.rem(x + d, 4) * 8 + s * 2
                else:
                    slot = lev * 32 + s * 8 + lax.rem(y + d, 4) * 2 + 1
                mine = iota((8, 128), 0) * 128 + iota((8, 128), 1) == slot
                p = jnp.sum(jnp.where(mine, pairs[...], 0).astype(F32), keepdims=True).astype(jnp.int32)
                limit[h, role, s] = NDEG - jnp.broadcast_to(p, (1, ROWS))
    vert_copy.wait()
    row = iota((128, 64), 0)
    q, k = row >> 5, (row >> 2) & 3
    e = jnp.where(q == 0, 14, jnp.where(q == 1, 12, jnp.where(q == 2, 4, 6))) + k
    e = e + jnp.where(((q == 1) | (q == 2)) & (k >= 2), 4, 0)
    level = ((lev + 32 - e) & 15) * 4 + (row & 3)
    chosen = (level == iota((128, 64), 1)).astype(BF16)
    both = jnp.concatenate([vert[...], vert[...]], axis=0)
    twice = lax.dot_general(chosen, both, (((1,), (1,)), ((), ())), preferred_element_type=F32)
    same = ((iota((128, 128), 0) >> 4) & 1) == (iota((128, 128), 1) >> 6)
    wide[...] = jnp.where(same, twice, F32(0.0)).astype(BF16)

    def summed(q, h, n, s, role):
        g = mixed[q, pl.ds(pl.multiple_of(s * 64, 64), 64), pl.ds(pl.multiple_of((2 * h + n) * 128, 128), 256)]
        both = jnp.dot(g, legs[h, n, s].reshape(256, ROWS), preferred_element_type=F32)
        return jnp.where(iota((32, ROWS), 1) < limit[h, role, s], both[0:32], both[32:64])

    out_copies = {}

    def arrive(q):
        for k in range(4):
            if (q, k) in z_copies:
                z_copies[q, k].wait_recv()
                z_copies[q, k].wait_send()
        mixed[q] = jnp.dot(spread[...], zr[q].reshape(256, 640), preferred_element_type=F32).astype(BF16)

    def step_copy(q, h, s):
        return pltpu.make_async_remote_copy(
            src_ref=t1.at[q, h, s], dst_ref=r1.at[q, h, s],
            send_sem=ts_sem.at[q, h, s], recv_sem=tr_sem.at[q, h, s],
            device_id=at(h, 3 - 2 * (s & 1)), device_id_type=MESH)

    def step_on(q, h, s):
        t1[q, h, s] = summed(q, h, 1 - (s & 1), s, 0).astype(BF16)
        step_copy(q, h, s).start()

    def place(h, d):
        return lax.rem((y if h == 0 else x) + d, 4)

    def step_all(q):
        for d in (2, 1, 3, 0):
            for h in range(2):
                step_on(q, h, place(h, d))

    def send(q, h, k, part, value):
        rs[q, h, k, part] = value.astype(BF16)
        step = (1, 1, 3)[k] if k > 0 else (1, 3)[part]
        copy = pltpu.make_async_remote_copy(
            src_ref=rs.at[q, h, k, part], dst_ref=rr.at[q, h, k, part],
            send_sem=rs_sem.at[q, h, k, part], recv_sem=rr_sem.at[q, h, k, part],
            device_id=at(1 - h, step), device_id_type=MESH)
        copy.start()
        out_copies[q, h, k, part] = copy

    def line(q):
        for d in (2, 1, 3, 0):
            for h in range(2):
                s = place(h, d)
                step_copy(q, h, s).wait_recv()
                value = summed(q, h, s & 1, s, 1) + r1[q, h, s].astype(F32)
                if d == 2:
                    send(q, h, 0, 0, value[:, 0:HALF])
                    send(q, h, 0, 1, value[:, HALF:ROWS])
                elif d == 1:
                    send(q, h, 1, 1, value[:, HALF:ROWS])
                    keep[q, h, 0] = value[:, 0:HALF]
                elif d == 3:
                    send(q, h, 2, 0, value[:, 0:HALF])
                    keep[q, h, 1] = value[:, HALF:ROWS]
                else:
                    own[q, h] = value

    def merge(q):
        for part in range(2):
            for h in range(2):
                out_copies[q, h, 0, part].wait()
                send(q, h, 1 + part, part, keep[q, h, part] + rr[q, h, 0, part].astype(F32))

    def finish(q):
        for h in range(2):
            for part in range(2):
                lanes = slice(part * HALF, (part + 1) * HALF)
                value = own[q, h, :, lanes]
                for k in (1, 2):
                    out_copies[q, h, k, part].wait()
                    value = value + rr[q, h, k, part].astype(F32)
                total[h, q * 32:(q + 1) * 32, lanes] = value.astype(BF16)

    arrive(0)
    arrive(1)
    for s in range(4):
        for copy in local[4 * s:4 * s + 4] + remote[4 * s:4 * s + 4]:
            copy.wait()
        for q in range(2):
            for h in range(2):
                step_on(q, h, s)
    line(0)
    line(1)
    merge(0)
    merge(1)
    arrive(2)
    step_all(2)
    arrive(3)
    step_all(3)
    finish(0)
    finish(1)
    line(2)
    line(3)
    merge(2)
    merge(3)
    finish(2)
    finish(3)
    for q in range(4):
        for h in range(2):
            for s in range(4):
                step_copy(q, h, s).wait_send()
    for h in range(2):
        for r in range(0, ROWS, 256):
            coef = total[h, :, r:r + 256].astype(F32).T.astype(BF16)
            out[0, h, r:r + 256, :] = jnp.dot(coef, wide[...], preferred_element_type=F32).astype(BF16)


def body(grid, pair_index, legendre, vertical):
    vmem = pl.BlockSpec(memory_space=pltpu.VMEM)
    hbm = pl.BlockSpec(memory_space=pl.ANY)
    dma = pltpu.SemaphoreType.DMA
    return pl.pallas_call(
        kernel,
        out_shape=jax.ShapeDtypeStruct((1, 2, ROWS, 128), BF16),
        in_specs=[hbm, hbm, hbm, hbm],
        out_specs=vmem,
        scratch_shapes=[
            pltpu.VMEM((4, 80, NLON), BF16),
            pltpu.VMEM((64, 64), BF16),
            pltpu.VMEM((320, NLON // 2), BF16),
            pltpu.VMEM((320, NLON // 2), BF16),
            pltpu.VMEM((8, 128), jnp.int32),
            pltpu.VMEM((2, 2, 4, 1, ROWS), jnp.int32),
            pltpu.VMEM((2, 2, NLON // 2, 256), BF16),
            pltpu.VMEM((2, 2, 24, 128), F32),
            pltpu.VMEM((2, 2, 24, 128), F32),
            pltpu.VMEM((2, 2, 2, 4, 80, 128), BF16),
            pltpu.VMEM((2, 4, 8, 80, 128), BF16),
            pltpu.VMEM((128, 128), BF16),
            pltpu.VMEM((256, 256), BF16),
            pltpu.VMEM((2, 8, 4, 16, 640), BF16),
            pltpu.VMEM((4, 4, 4, 16, 640), BF16),
            pltpu.VMEM((4, 256, 640), BF16),
            pltpu.VMEM((2, 2, 4, 16, 16, ROWS), BF16),
            pltpu.VMEM((4, 2, 4, 32, ROWS), BF16),
            pltpu.VMEM((4, 2, 4, 32, ROWS), BF16),
            pltpu.VMEM((4, 2, 3, 2, 32, HALF), BF16),
            pltpu.VMEM((4, 2, 3, 2, 32, HALF), BF16),
            pltpu.VMEM((4, 2, 2, 32, HALF), F32),
            pltpu.VMEM((4, 2, 32, ROWS), F32),
            pltpu.VMEM((2, 128, ROWS), BF16),
            pltpu.VMEM((128, 128), BF16),
            dma((3,)), dma((2, 2, 4)), dma((2, 2, 4)), dma((2, 2, 4)), dma((2, 2, 2)), dma((2, 2, 2)),
            dma((4, 4)), dma((4, 4)), dma((4, 2, 4)), dma((4, 2, 4)), dma((4, 2, 3, 2)), dma((4, 2, 3, 2)),
        ],
        compiler_params=pltpu.CompilerParams(
            collective_id=0, has_side_effects=True, vmem_limit_bytes=VMEM_MIB * 1024 * 1024),
        cost_estimate=pl.CostEstimate(flops=8_000_000_000, bytes_accessed=12_000_000, transcendentals=0),
        name="spectral",
    )(legendre.reshape(4, 4, 2, 5, 16, ROWS), grid, pair_index.reshape(4, 128), vertical)


def solution(mesh):
    placed = (P("lev", "lat", None), P(), P("lev", "lat", None), P())
    return jax.shard_map(
        body, mesh=mesh, in_specs=placed, out_specs=P("lev", "lat", None, None), check_vma=False
    )
```
